128 devices in a mesh: layer: 2 (over x_lo), row: 2 (over x_hi), col: 32 (over z, y, core).
Axes of the slice: x: 4 (x_hi: 2, x_lo: 2; x = x_hi * 2 + x_lo), y: 4, z: 4, core: 2. Of those that a mesh axis runs over, the one named last changes fastest.
Arguments:
- values: bfloat16 [8192, 8192], P('row', ('layer', 'col'))
- pattern: int32 [64, 64], replicated, may hold values from 0 to 1, as said below
- keep_square: int32 [64, 64], replicated, may hold values from 0 to 1, as said below
- keep_next: int32 [64, 64], replicated, may hold values from 0 to 1, as said below
Outputs:
- square: bfloat16 [8192, 8192], P('row', ('layer', 'col'))
- next_sign: bfloat16 [8192, 8192], P('row', ('layer', 'col'))
The draws below stay inside these ranges and needn't reach their ends.
Inputs may be any that keep to these rules, and one draw needn't show every extreme that they name: `pattern`: 0 or 1; every diagonal block is 1; the number of 1 block differs from block row to block row. `keep_square`: 0 or 1; every diagonal block is 1. `keep_next`: 0 or 1; every diagonal block is 1.
All inputs are finite; a program needn't handle non-finite values.
Results may differ from the reference program's by a relative error of at most 0.0018.
Values may be sent and summed in bfloat16 or wider, within the bound.
No kernel may reach another device: no remote copies, remote signals or barrier semaphores. Data moves between devices by JAX's collectives and lax.ppermute only.
A program may use at most 128 MiB of HBM per device.

```python
import math
import jax
import jax.numpy as jnp

TILE = 128
ORDER = 8192
BLOCKS = 64


reach_limit = 6


def banded(base_key, widen):
    block_index = jnp.arange(BLOCKS)
    apart = jnp.abs(block_index[:, None] - block_index[None, :])
    apart = jnp.minimum(apart, BLOCKS - apart)
    reach_most = max(1, min(reach_limit, BLOCKS // 8)) * widen
    reach_row = jax.random.randint(jax.random.fold_in(base_key, 11), (BLOCKS, 1), 1, reach_most + 1)
    distant = jax.random.randint(jax.random.fold_in(base_key, 12), (BLOCKS, BLOCKS), 0, 16) == 0
    return jnp.where((apart <= reach_row) | distant, 1, 0).astype(jnp.int32)


def draw_values(key, part):
    key = jax.random.fold_in(key, 1)
    spread = 0.4 / math.sqrt(TILE * 8.0)
    normal_key = jax.random.fold_in(key, 21)
    size_key = jax.random.fold_in(key, 22)
    signs_key = jax.random.fold_in(key, 23)
    scattered = jax.random.normal(normal_key, (ORDER, ORDER), jnp.float32) * spread
    magnitude = jax.random.uniform(size_key, (ORDER,), jnp.float32, 0.2, 0.6)
    signs = jax.random.randint(signs_key, (ORDER,), 0, 2).astype(jnp.float32) * 2.0 - 1.0
    positions = jnp.arange(ORDER)
    on_diagonal = positions[:, None] == positions[None, :]
    return jnp.where(on_diagonal, (magnitude * signs)[:, None], scattered).astype(jnp.bfloat16)


def draw_pattern(key, part):
    key = jax.random.fold_in(key, 2)
    return banded(key, 1)


def draw_keep_square(key, part):
    key = jax.random.fold_in(key, 3)
    return banded(key, 2)


def draw_keep_next(key, part):
    key = jax.random.fold_in(key, 4)
    return banded(key, 3)


def setup_inputs(seed: int = 0) -> dict:
    seeds = jax.random.split(jax.random.key(seed), 5)
    return {
        "values": draw_values(jax.random.fold_in(seeds[4], 71), 0),
        "pattern": draw_pattern(jax.random.fold_in(seeds[4], 71), 0),
        "keep_square": draw_keep_square(jax.random.fold_in(seeds[4], 71), 0),
        "keep_next": draw_keep_next(jax.random.fold_in(seeds[4], 71), 0),
    }


def tile_mask(matrix, mask_tiles):
    row_tiles, col_tiles = mask_tiles.shape
    shaped = matrix.reshape(row_tiles, TILE, col_tiles, TILE)
    return (shaped * mask_tiles[:, None, :, None].astype(matrix.dtype)).reshape(matrix.shape)


def reference(values, pattern, keep_square, keep_next):
    start_matrix = tile_mask(values, pattern)
    square_raw = jnp.dot(start_matrix, start_matrix, preferred_element_type=jnp.float32)
    square = tile_mask(square_raw, keep_square).astype(jnp.bfloat16)
    product = jnp.dot(start_matrix, square, preferred_element_type=jnp.float32)
    update = 1.5 * start_matrix.astype(jnp.float32) - 0.5 * product
    next_sign = tile_mask(update, keep_next).astype(jnp.bfloat16)
    return square, next_sign
```

```python
import functools

import jax
import jax.numpy as jnp
from jax import lax
from jax.experimental import pallas as pl
from jax.experimental.pallas import tpu as pltpu
from jax.sharding import PartitionSpec as P

TILE = 128
SHIFT = 10
MASK = (1 << SHIFT) - 1
BF16 = jnp.bfloat16
F32 = jnp.float32
HALF, SENT = 18, 11
TIERS = ((12, 34, 16), (16, 46, 20))
VMEM_LIMIT = 60 * 1024 * 1024


def spread(value, axis, root):
    mine = lax.axis_index(axis) == root
    return lax.psum(jnp.where(mine, value, jnp.zeros_like(value)), axis)


def tile_mask(matrix, mask_tiles):
    row_tiles, col_tiles = mask_tiles.shape
    shaped = matrix.reshape(row_tiles, TILE, col_tiles, TILE)
    return (shaped * mask_tiles[:, None, :, None].astype(matrix.dtype)).reshape(matrix.shape)


def dense(values, pattern, keep_square, keep_next):
    col_count = lax.axis_size("col")
    layer_index = lax.axis_index("layer")
    row_index = lax.axis_index("row")
    col_index = lax.axis_index("col")
    row_count, piece_width = values.shape
    row_tiles = row_count // TILE
    col_tiles = piece_width // TILE
    first_row = row_index * row_tiles
    first_col = (layer_index * col_count + col_index) * col_tiles

    def local_mask(mask_whole):
        return lax.dynamic_slice(mask_whole, (first_row, first_col), (row_tiles, col_tiles))

    start_matrix = tile_mask(values, local_mask(pattern))
    left_whole = lax.all_gather(start_matrix, "col", axis=1, tiled=True)

    def column_block(matrix):
        gathered = lax.all_gather(matrix, "layer", axis=1, tiled=True)
        return spread(gathered, "row", layer_index)

    def multiply(right_block):
        layer_part = jnp.dot(left_whole, right_block, preferred_element_type=jnp.float32)
        summed = lax.psum(layer_part, "layer")
        return lax.dynamic_slice_in_dim(summed, layer_index * piece_width, piece_width, 1)

    square_raw = multiply(column_block(start_matrix))
    square = tile_mask(square_raw, local_mask(keep_square)).astype(jnp.bfloat16)
    product = multiply(column_block(square))
    update = 1.5 * start_matrix.astype(jnp.float32) - 0.5 * product
    next_sign = tile_mask(update, local_mask(keep_next)).astype(jnp.bfloat16)
    return (square, next_sign)


def shift_x(value, by):
    def flat(x):
        return x % 2 * 2 + x // 2

    return lax.ppermute(value, ("layer", "row"), [(flat(x), flat((x + by) % 4)) for x in range(4)])


def shift_ring(value, by, stage):
    def target(c):
        z, y, core = c // 8, c // 2 % 4, c % 2
        if core == stage:
            y = (y + by) % 4
        else:
            z = (z + by) % 4
        return z * 8 + y * 2 + core

    return lax.ppermute(value, "col", [(c, target(c)) for c in range(32)])


def swap_core(value):
    return lax.ppermute(value, "col", [(c, c ^ 1) for c in range(32)])


def swap_layer(value):
    return lax.ppermute(value, "layer", [(0, 1), (1, 0)])


def after(value, *others):
    return lax.optimization_barrier((value, *others))[0]


def blocks_of(count):
    return jax.ShapeDtypeStruct((count * TILE, TILE), BF16)


def at_block(index):
    return pl.ds(pl.multiple_of(index * TILE, TILE), TILE)


ANY = pl.BlockSpec(memory_space=pl.ANY)
VMEM = pl.BlockSpec(memory_space=pltpu.VMEM)


def fetch(sources, offsets, scratch, sems):
    copies = [
        pltpu.make_async_copy(src, scratch.at[pl.ds(off * TILE, src.shape[0])], sems.at[n])
        for n, (src, off) in enumerate(zip(sources, offsets, strict=True))
    ]
    for copy in copies:
        copy.start()
    return copies


def offsets_of(arrays):
    offsets, total = [], 0
    for a in arrays:
        offsets.append(total)
        total += a.shape[0] // TILE
    return offsets, total


def pack_column(pattern, values):
    def kernel(pattern_ref, values_ref, own_ref, sent_ref):
        layer = lax.axis_index("layer")
        first = lax.axis_index("row") * 32
        column = layer * 32 + lax.axis_index("col")

        def step(a, counts):
            n, m = counts
            for s in range(2):
                t = 2 * a + s
                keep = pattern_ref[first + t, column]

                @pl.when((keep != 0) & (n < HALF))
                def _(n=n, t=t):
                    own_ref[at_block(n), :] = values_ref[at_block(t), :]

                @pl.when((keep != 0) & (m < SENT) & (layer != s))
                def _(m=m, t=t):
                    sent_ref[at_block(m), :] = values_ref[at_block(t), :]

                n = n + keep
                m = m + jnp.where(layer != s, keep, 0)
            return n, m

        lax.fori_loop(0, 16, step, (0, 0))

    return pl.pallas_call(
        kernel,
        grid_spec=pltpu.PrefetchScalarGridSpec(
            num_scalar_prefetch=1, grid=(), in_specs=[VMEM], out_specs=[VMEM, VMEM]),
        out_shape=[blocks_of(HALF), blocks_of(SENT)],
        compiler_params=pltpu.CompilerParams(vmem_limit_bytes=VMEM_LIMIT),
        name="pack_column",
    )(pattern, values)


def repack(index, sources, caps, name):
    offsets, total = offsets_of(sources)
    count = len(sources)

    def kernel(index_ref, *refs):
        srcs, outs = refs[:count], refs[count : count + len(caps)]
        scratch, sems = refs[count + len(caps) :]
        for copy in fetch(srcs, offsets, scratch, sems):
            copy.wait()
        base = 0
        for out, cap in zip(outs, caps, strict=True):
            for p in range(cap):
                out[pl.ds(p * TILE, TILE), :] = scratch[at_block(index_ref[base + p]), :]
            base += cap

    return pl.pallas_call(
        kernel,
        grid_spec=pltpu.PrefetchScalarGridSpec(
            num_scalar_prefetch=1, grid=(), in_specs=[ANY] * count, out_specs=[VMEM] * len(caps),
            scratch_shapes=[pltpu.VMEM((total * TILE, TILE), BF16), pltpu.SemaphoreType.DMA((count,))]),
        out_shape=[blocks_of(cap) for cap in caps],
        compiler_params=pltpu.CompilerParams(vmem_limit_bytes=VMEM_LIMIT),
        name=name,
    )(index, *sources)


def sum_of_products(row, list_ref, count, left, right):
    def step(i, total):
        for u in range(4):
            code = list_ref[row, i * 4 + u]
            a = left[at_block(code >> SHIFT), :]
            b = right[at_block(code & MASK), :]
            total += jnp.dot(a, b, preferred_element_type=F32)
        return total

    return lax.fori_loop(0, (count + 3) >> 2, step, jnp.zeros((TILE, TILE), F32))


def load_operands(left_srcs, right_srcs, left_offs, right_offs, left, right, sems):
    n = len(left_srcs)
    copies = fetch(left_srcs, left_offs, left, sems)
    copies += fetch(right_srcs, right_offs, right, sems.at[pl.ds(n, len(right_srcs))])
    zero = jnp.zeros((TILE, TILE), BF16)
    left[pl.ds(left.shape[0] - TILE, TILE), :] = zero
    right[pl.ds(right.shape[0] - TILE, TILE), :] = zero
    for copy in copies:
        copy.wait()


def square_blocks(lists, meta, lefts, rights, cap):
    left_offs, left_total = offsets_of(lefts)
    right_offs, right_total = offsets_of(rights)
    nl, nr = len(lefts), len(rights)

    def kernel(list_ref, meta_ref, *refs):
        out, left, right, sems = refs[nl + nr :]
        load_operands(refs[:nl], refs[nl : nl + nr], left_offs, right_offs, left, right, sems)

        def step(o, carry):
            @pl.when(meta_ref[1, o] != 0)
            def _():
                total = sum_of_products(o, list_ref, meta_ref[0, o], left, right)
                out[at_block(jnp.minimum(meta_ref[2, o], cap - 1)), :] = total.astype(BF16)

            return carry

        lax.fori_loop(0, 32, step, 0)

    return pl.pallas_call(
        kernel,
        grid_spec=pltpu.PrefetchScalarGridSpec(
            num_scalar_prefetch=2, grid=(), in_specs=[ANY] * (nl + nr), out_specs=VMEM,
            scratch_shapes=[
                pltpu.VMEM(((left_total + 1) * TILE, TILE), BF16),
                pltpu.VMEM(((right_total + 1) * TILE, TILE), BF16),
                pltpu.SemaphoreType.DMA((nl + nr,)),
            ]),
        out_shape=blocks_of(cap),
        compiler_params=pltpu.CompilerParams(vmem_limit_bytes=VMEM_LIMIT),
        name="square_blocks",
    )(lists, meta, *lefts, *rights)


def next_blocks(lists, meta, lefts, rights, own):
    left_offs, left_total = offsets_of(lefts)
    right_offs, right_total = offsets_of(rights)
    nl, nr = len(lefts), len(rights)
    n_out = 2 if own else 1

    def kernel(list_ref, meta_ref, *refs):
        outs = refs[nl + nr : nl + nr + n_out]
        left, right, sems = refs[nl + nr + n_out :]
        load_operands(refs[:nl], refs[nl : nl + nr], left_offs, right_offs, left, right, sems)
        layer = lax.axis_index("layer")
        column = layer if own else 1 - layer

        def step(a, carry):
            o = column * 16 + a
            outs[0][at_block(a), :] = jnp.zeros((TILE, TILE), BF16)

            @pl.when(meta_ref[1, o] != 0)
            def _():
                total = sum_of_products(o, list_ref, meta_ref[0, o], left, right)
                start = left[at_block(meta_ref[2, o]), :].astype(F32)
                outs[0][at_block(a), :] = (1.5 * start - 0.5 * total).astype(BF16)

            return carry

        lax.fori_loop(0, 16, step, 0)

        if own:
            def place(t, carry):
                slot = meta_ref[3, t]

                @pl.when(slot >= 0)
                def _():
                    outs[1][at_block(t), :] = right[at_block(slot), :]

                @pl.when(slot < 0)
                def _():
                    outs[1][at_block(t), :] = jnp.zeros((TILE, TILE), BF16)

                return carry

            lax.fori_loop(0, 32, place, 0)

    return pl.pallas_call(
        kernel,
        grid_spec=pltpu.PrefetchScalarGridSpec(
            num_scalar_prefetch=2, grid=(), in_specs=[ANY] * (nl + nr), out_specs=[VMEM] * n_out,
            scratch_shapes=[
                pltpu.VMEM(((left_total + 1) * TILE, TILE), BF16),
                pltpu.VMEM(((right_total + 1) * TILE, TILE), BF16),
                pltpu.SemaphoreType.DMA((nl + nr,)),
            ]),
        out_shape=[blocks_of(16)] + ([blocks_of(32)] if own else []),
        compiler_params=pltpu.CompilerParams(vmem_limit_bytes=VMEM_LIMIT),
        name="next_own" if own else "next_sent",
    )(lists, meta, *lefts, *rights)


def interleave(mine, other):
    def kernel(mine_ref, other_ref, out_ref):
        layer = lax.axis_index("layer")
        for a in range(16):
            out_ref[at_block(2 * a + layer), :] = mine_ref[pl.ds(a * TILE, TILE), :]
            out_ref[at_block(2 * a + 1 - layer), :] = other_ref[pl.ds(a * TILE, TILE), :]

    return pl.pallas_call(
        kernel,
        in_specs=[VMEM, VMEM],
        out_specs=VMEM,
        out_shape=blocks_of(32),
        compiler_params=pltpu.CompilerParams(vmem_limit_bytes=VMEM_LIMIT),
        name="interleave",
    )(mine, other)


def dot01(a, b):
    return jnp.dot(a.astype(BF16), b.astype(BF16), preferred_element_type=F32)


def dot01t(a, b):
    return lax.dot_general(a.astype(BF16), b.astype(BF16), (((1,), (1,)), ((), ())), preferred_element_type=F32)


def whole(value):
    return value.astype(jnp.int32)


def choose(hit, value, length, dest):
    slots = lax.broadcasted_iota(jnp.int32, (length, *value.shape), 0)
    return jnp.sum(jnp.where(hit[None] & (dest[None] == slots), value[None], 0), axis=tuple(range(1, value.ndim + 1)))


def iota(shape, dim):
    return lax.broadcasted_iota(jnp.int32, shape, dim)


def zz(k):
    return k % 32 // 8


def yy(k):
    return k % 8 // 2


def tier_of(pattern, keep_square):
    owner = (iota((4, 64), 1) // 32 == iota((4, 64), 0) // 2) & (iota((4, 64), 1) % 2 == iota((4, 64), 0) % 2)
    group = iota((64, 32), 0) % 32 == iota((64, 32), 1)
    c, ring = iota((32, 8), 0), iota((32, 8), 1)
    ring = (c % 2 == ring // 4) & (jnp.where(c % 2 == 0, zz(c), yy(c)) == ring % 4)
    counts = dot01(owner, pattern)
    sent = jnp.max(counts)
    half = jnp.maximum(jnp.max(counts[0] + counts[1]), jnp.max(counts[2] + counts[3]))
    chunks = dot01(counts, group)
    first, second = jnp.max(chunks), jnp.max(dot01(chunks, ring))
    third = jnp.max(dot01(dot01(owner, keep_square), group))
    which = jnp.int32(len(TIERS))
    for n in reversed(range(len(TIERS))):
        c1, c2, c3 = TIERS[n]
        which = jnp.where((first <= c1) & (second <= c2) & (third <= c3), n, which)
    return jnp.where((half <= HALF) & (sent <= SENT), which, len(TIERS)).astype(jnp.int32)


def tables(pattern, keep_square, keep_next, tier):
    c1, c2, c3 = [jnp.where(tier == 0, a, b) for a, b in zip(*TIERS, strict=True)]
    most1, most2 = [max(t[n] for t in TIERS) for n in range(2)]
    layer, row, col = lax.axis_index("layer"), lax.axis_index("row"), lax.axis_index("col")
    z, y, core, x = col // 8, col // 2 % 4, col % 2, row * 2 + layer
    i, k = iota((64, 64), 0), iota((64, 64), 1)
    a16, k16 = iota((16, 64), 0), iota((16, 64), 1)
    j2, k2 = iota((2, 64), 0), iota((2, 64), 1)
    rowsel = k16 == row * 32 + a16 * 2 + layer
    colsel = j2 * 32 + col == k2
    rank0 = dot01((i // 32 == k // 32) & (k < i), pattern)
    rows = dot01(rowsel, pattern)
    cols = dot01t(colsel, pattern)
    col_rank0 = whole(dot01t(colsel, rank0))
    has = rows > 0

    below = iota((16, 16), 1) < iota((16, 16), 0)
    sent_rank = whole(dot01(below, rows))
    group_count = dot01(rows, i % 32 == k % 32)
    rank1 = whole(dot01(below, group_count) + dot01(rows, (i % 32 == k % 32) & (i < k)))
    n1 = jnp.sum(group_count, axis=0, keepdims=True)
    before = jnp.where(k % 2 == 0, (zz(i) == zz(k)) & (yy(i) < yy(k)), (yy(i) == yy(k)) & (zz(i) < zz(k)))
    rank2 = rank1 + whole(dot01(n1, before & (i < 32) & (i % 2 == k % 2)))
    ez, ey = (zz(k16) - z) % 4, (yy(k16) - y) % 4
    even = k16 % 2 == 0
    slot_left = jnp.where(even, ez, ey) * c2 + jnp.where(k16 % 2 == core, 0, 4 * c2) + rank2
    list1 = choose(has & (k16 % 32 == col), jnp.where(k16 // 32 == layer, a16 * 2 + layer, 32 + sent_rank), most1, rank1)
    list2 = choose(
        has & (k16 % 2 == core) & (jnp.where(even, ez, ey) == 0),
        jnp.where(even, ey, ez) * c1 + rank1,
        most2,
        rank2,
    )

    slot_right = (k2 // 32 * 2 + j2 - x) % 4 * HALF + col_rank0
    kept = dot01t(colsel, keep_square)
    g3 = dot01(kept, (i // 32 == k // 32) & (i % 2 == k % 2) & (i < k))
    rank3 = jnp.sum(g3, axis=0, keepdims=True) + jnp.where(j2 == 1, kept[:1], 0)
    slot_square = (k2 // 32 * 2 + k2 % 2 - x) % 4 * c3 + whole(rank3)
    keep_mine = dot01t(kept, rowsel)
    next_mine = dot01t(dot01t(colsel, keep_next), rowsel)
    place3 = whole(dot01t(rank3, rowsel))
    nothing_left = 8 * c2

    def pairs(right_has, keep, right_slots, nothing_right):
        hit = (rows[None] * right_has[:, None] * keep[:, :, None]).reshape(32, 64)
        rank = whole(dot01(hit, i < k))
        nothing = (nothing_left << SHIFT) + nothing_right
        code = ((slot_left[None] << SHIFT) + right_slots[:, None]).reshape(32, 64) - nothing
        where = (hit[:, None] > 0) & (rank[:, None] == iota((32, 64, 64), 1))
        return jnp.sum(jnp.where(where, code[:, None], 0), axis=2) + nothing, whole(jnp.sum(hit, axis=1))

    square_list, square_count = pairs(cols, keep_mine, slot_right, 4 * HALF)
    next_list, next_count = pairs(kept, next_mine, slot_square, 4 * c3)
    square_meta = jnp.stack([square_count, whole(keep_mine).reshape(32), place3.reshape(32)])
    start = jnp.sum(jnp.where(colsel[:, None] & has[None], slot_left[None] - nothing_left, 0), axis=2) + nothing_left
    own = jnp.where(kept > 0, slot_square, -1)
    own = jnp.where(layer == 0, own[0], own[1])
    own = lax.dynamic_slice(own, (row * 32,), (32,))
    next_meta = jnp.stack([next_count, whole(next_mine).reshape(32), start.reshape(32), own])
    return list1, list2, square_list, square_meta, next_list, next_meta


def packed(caps, values, pattern, keep_square, keep_next, own, received, *lists):
    c1, c2, c3 = caps
    list1, list2, square_list, square_meta, next_list, next_meta = lists

    with jax.named_scope("left_rows"):
        (chunk,) = repack(list1, [values, received], [c1], "pack_rows")
        chunks = [chunk] + [shift_ring(chunk, -e, 0) for e in (1, 2, 3)]
        (ring,) = repack(list2, chunks, [c2], "pack_ring")
        rings = [ring] + [shift_ring(ring, -e, 1) for e in (1, 2, 3)]
        lefts = rings + [swap_core(v) for v in rings]
    with jax.named_scope("right_columns"):
        rights = [own] + [shift_x(after(own, chunk), -e) for e in (1, 2, 3)]
    with jax.named_scope("square"):
        sq = square_blocks(square_list, square_meta, lefts, rights, c3)
        squares = [sq] + [shift_x(sq, -e) for e in (1, 2, 3)]
    with jax.named_scope("next"):
        (sent,) = next_blocks(next_list, next_meta, lefts, squares, False)
        other = swap_layer(sent)
        mine, square = next_blocks(next_list, next_meta, lefts, squares, True)
        next_sign = interleave(mine, other)
    return (square, next_sign)


def local(values, pattern, keep_square, keep_next):
    own, sent = pack_column(pattern, values)
    received = swap_layer(sent)
    tier = tier_of(pattern, keep_square)
    lists = tables(pattern, keep_square, keep_next, tier)

    def without_lists(*args):
        return dense(*args[:4])

    branches = [functools.partial(packed, caps) for caps in TIERS] + [without_lists]
    return lax.switch(tier, branches, values, pattern, keep_square, keep_next, own, received, *lists)


def solution(mesh):
    return jax.shard_map(
        local,
        mesh=mesh,
        in_specs=(P("row", ("layer", "col")), P(), P(), P()),
        out_specs=(P("row", ("layer", "col")), P("row", ("layer", "col"))),
        check_vma=False,
    )
```

```python
import functools

import jax
import jax.numpy as jnp
from jax import lax
from jax.experimental import pallas as pl
from jax.experimental.pallas import tpu as pltpu
from jax.sharding import PartitionSpec as P

TILE = 128
SHIFT = 10
MASK = (1 << SHIFT) - 1
BF16 = jnp.bfloat16
F32 = jnp.float32
TIERS = ((18, 11, 14, 38, 18), (32, 16, 32, 128, 32))
VMEM_LIMIT = 20 * 1024 * 1024


def shift_ring(value, by, stage):
    def target(c):
        z, y, core = c // 8, c // 2 % 4, c % 2
        if core == stage:
            y = (y + by) % 4
        else:
            z = (z + by) % 4
        return z * 8 + y * 2 + core

    return lax.ppermute(value, "col", [(c, target(c)) for c in range(32)])


def carry_x(value):
    def target(i):
        layer, row, col = i // 64, i // 32 % 2, i % 32
        x = (row * 2 + layer + (1 if col % 2 == 0 else -1)) % 4
        return x % 2 * 64 + x // 2 * 32 + col

    return lax.ppermute(value, ("layer", "row", "col"), [(i, target(i)) for i in range(128)])


def gather_x(value):
    carried = carry_x(value)
    crossed = carry_x(swap_core(value))
    return [value, carried, carry_x(carried), swap_core(crossed)]


def place_x(x, e, core):
    return jnp.where(core == 0, (4 - e) % 4, e)


def swap_core(value):
    return lax.ppermute(value, "col", [(c, c ^ 1) for c in range(32)])


def swap_layer(value):
    return lax.ppermute(value, "layer", [(0, 1), (1, 0)])


def after(value, *others):
    return lax.optimization_barrier((value, *others))[0]


def blocks_of(count):
    return jax.ShapeDtypeStruct((count * TILE, TILE), BF16)


def at_block(index):
    return pl.ds(pl.multiple_of(index * TILE, TILE), TILE)


ANY = pl.BlockSpec(memory_space=pl.ANY)
VMEM = pl.BlockSpec(memory_space=pltpu.VMEM)


def fetch(sources, offsets, scratch, sems):
    copies = [
        pltpu.make_async_copy(src, scratch.at[pl.ds(off * TILE, src.shape[0])], sems.at[n])
        for n, (src, off) in enumerate(zip(sources, offsets, strict=True))
    ]
    for copy in copies:
        copy.start()
    return copies


def offsets_of(arrays):
    offsets, total = [], 0
    for a in arrays:
        offsets.append(total)
        total += a.shape[0] // TILE
    return offsets, total


def pack_column(pattern, values, half, part):
    def kernel(pattern_ref, values_ref, own_ref, sent_ref):
        layer = lax.axis_index("layer")
        first = lax.axis_index("row") * 32
        column = layer * 32 + lax.axis_index("col")

        def step(a, counts):
            n, m = counts
            for s in range(2):
                t = 2 * a + s
                keep = pattern_ref[first + t, column]

                @pl.when((keep != 0) & (n < half))
                def _(n=n, t=t):
                    own_ref[at_block(n), :] = values_ref[at_block(t), :]

                @pl.when((keep != 0) & (m < part) & (layer != s))
                def _(m=m, t=t):
                    sent_ref[at_block(m), :] = values_ref[at_block(t), :]

                n = n + keep
                m = m + jnp.where(layer != s, keep, 0)
            return n, m

        lax.fori_loop(0, 16, step, (0, 0))

    return pl.pallas_call(
        kernel,
        grid_spec=pltpu.PrefetchScalarGridSpec(
            num_scalar_prefetch=1, grid=(), in_specs=[VMEM], out_specs=[VMEM, VMEM]),
        out_shape=[blocks_of(half), blocks_of(part)],
        compiler_params=pltpu.CompilerParams(vmem_limit_bytes=VMEM_LIMIT),
        name="pack_column",
    )(pattern, values)


def pack_rows(pattern, values, received, cap):
    def kernel(pattern_ref, values_ref, received_ref, out_ref):
        layer = lax.axis_index("layer")
        first = lax.axis_index("row") * 32 + layer
        col = lax.axis_index("col")
        count = lax.fori_loop(0, 16, lambda a, n: n + pattern_ref[first + 2 * a, (1 - layer) * 32 + col], 0, unroll=4)

        def step(a, n):
            keep = pattern_ref[first + 2 * a, layer * 32 + col]

            @pl.when((keep != 0) & (n < cap))
            def _():
                out_ref[at_block(n), :] = values_ref[at_block(2 * a + layer), :]

            return n + keep

        end = lax.fori_loop(0, 16, step, jnp.where(layer == 0, 0, count))
        base = jnp.where(layer == 0, end, 0)

        def copy(n, carry):
            out_ref[at_block(base + n), :] = received_ref[at_block(n), :]
            return carry

        lax.fori_loop(0, jnp.minimum(count, cap - base), copy, 0)

    return pl.pallas_call(
        kernel,
        grid_spec=pltpu.PrefetchScalarGridSpec(
            num_scalar_prefetch=1, grid=(), in_specs=[VMEM, VMEM], out_specs=VMEM),
        out_shape=blocks_of(cap),
        compiler_params=pltpu.CompilerParams(vmem_limit_bytes=VMEM_LIMIT),
        name="pack_rows",
    )(pattern, values, received)


def pack_ring(info, chunks, cap):
    def kernel(info_ref, *refs):
        out = refs[4]
        for e in range(4):
            def copy(n, carry, e=e):
                place = jnp.minimum(info_ref[e, 2] + n, cap - 1)
                out[at_block(place), :] = refs[e][at_block(n), :]
                return carry

            lax.fori_loop(0, info_ref[e, 1], copy, 0)

    return pl.pallas_call(
        kernel,
        grid_spec=pltpu.PrefetchScalarGridSpec(
            num_scalar_prefetch=1, grid=(), in_specs=[VMEM] * 4, out_specs=VMEM),
        out_shape=blocks_of(cap),
        compiler_params=pltpu.CompilerParams(vmem_limit_bytes=VMEM_LIMIT),
        name="pack_ring",
    )(info, *chunks)


def sum_of_products(row, list_ref, count, left, right):
    def step(i, total):
        codes = [list_ref[row, i * 4 + u] for u in range(4)]
        a = jnp.concatenate([left[at_block(c >> SHIFT), :] for c in codes], axis=1)
        b = jnp.concatenate([right[at_block(c & MASK), :] for c in codes], axis=0)
        return total + jnp.dot(a, b, preferred_element_type=F32)

    return lax.fori_loop(0, (count + 3) >> 2, step, jnp.zeros((TILE, TILE), F32))


def vmem_for(blocks):
    return blocks * TILE * TILE * 2 + 6 * 1024 * 1024


def load_operands(left_srcs, right_srcs, left_offs, right_offs, left, right, sems):
    n = len(left_srcs)
    copies = fetch(left_srcs, left_offs, left, sems)
    copies += fetch(right_srcs, right_offs, right, sems.at[pl.ds(n, len(right_srcs))])
    zero = jnp.zeros((TILE, TILE), BF16)
    left[pl.ds(left.shape[0] - TILE, TILE), :] = zero
    right[pl.ds(right.shape[0] - TILE, TILE), :] = zero
    for copy in copies:
        copy.wait()


def square_blocks(lists, lefts, rights, cap):
    left_offs, left_total = offsets_of(lefts)
    right_offs, right_total = offsets_of(rights)
    nl, nr = len(lefts), len(rights)

    def kernel(list_ref, *refs):
        out, left, right, sems = refs[nl + nr :]
        load_operands(refs[:nl], refs[nl : nl + nr], left_offs, right_offs, left, right, sems)

        def step(o, carry):
            @pl.when(list_ref[o, 65] != 0)
            def _():
                total = sum_of_products(o, list_ref, list_ref[o, 64], left, right)
                out[at_block(jnp.minimum(list_ref[o, 66], cap - 1)), :] = total.astype(BF16)

            return carry

        lax.fori_loop(0, 32, step, 0)

    return pl.pallas_call(
        kernel,
        grid_spec=pltpu.PrefetchScalarGridSpec(
            num_scalar_prefetch=1, grid=(), in_specs=[ANY] * (nl + nr), out_specs=VMEM,
            scratch_shapes=[
                pltpu.VMEM(((left_total + 1) * TILE, TILE), BF16),
                pltpu.VMEM(((right_total + 1) * TILE, TILE), BF16),
                pltpu.SemaphoreType.DMA((nl + nr,)),
            ]),
        out_shape=blocks_of(cap),
        compiler_params=pltpu.CompilerParams(vmem_limit_bytes=vmem_for(left_total + right_total)),
        name="square_blocks",
    )(lists, *lefts, *rights)


def next_blocks(lists, lefts, rights, own):
    left_offs, left_total = offsets_of(lefts)
    right_offs, right_total = offsets_of(rights)
    nl, nr = len(lefts), len(rights)
    n_out = 2 if own else 1

    def kernel(list_ref, *refs):
        outs = refs[nl + nr : nl + nr + n_out]
        left, right, sems = refs[nl + nr + n_out :]
        load_operands(refs[:nl], refs[nl : nl + nr], left_offs, right_offs, left, right, sems)
        layer = lax.axis_index("layer")
        column = layer if own else 1 - layer

        def step(a, carry):
            o = column * 16 + a
            outs[0][at_block(a), :] = jnp.zeros((TILE, TILE), BF16)

            @pl.when(list_ref[o, 65] != 0)
            def _():
                total = sum_of_products(o, list_ref, list_ref[o, 64], left, right)
                start = left[at_block(list_ref[o, 66]), :].astype(F32)
                outs[0][at_block(a), :] = (1.5 * start - 0.5 * total).astype(BF16)

            return carry

        lax.fori_loop(0, 16, step, 0)

        if own:
            def place(t, carry):
                slot = list_ref[t, 67]

                @pl.when(slot >= 0)
                def _():
                    outs[1][at_block(t), :] = right[at_block(slot), :]

                @pl.when(slot < 0)
                def _():
                    outs[1][at_block(t), :] = jnp.zeros((TILE, TILE), BF16)

                return carry

            lax.fori_loop(0, 32, place, 0)

    return pl.pallas_call(
        kernel,
        grid_spec=pltpu.PrefetchScalarGridSpec(
            num_scalar_prefetch=1, grid=(), in_specs=[ANY] * (nl + nr), out_specs=[VMEM] * n_out,
            scratch_shapes=[
                pltpu.VMEM(((left_total + 1) * TILE, TILE), BF16),
                pltpu.VMEM(((right_total + 1) * TILE, TILE), BF16),
                pltpu.SemaphoreType.DMA((nl + nr,)),
            ]),
        out_shape=[blocks_of(16)] + ([blocks_of(32)] if own else []),
        compiler_params=pltpu.CompilerParams(vmem_limit_bytes=vmem_for(left_total + right_total)),
        name="next_own" if own else "next_sent",
    )(lists, *lefts, *rights)


def interleave(mine, other):
    def kernel(mine_ref, other_ref, out_ref):
        layer = lax.axis_index("layer")
        for a in range(16):
            out_ref[at_block(2 * a + layer), :] = mine_ref[pl.ds(a * TILE, TILE), :]
            out_ref[at_block(2 * a + 1 - layer), :] = other_ref[pl.ds(a * TILE, TILE), :]

    return pl.pallas_call(
        kernel,
        in_specs=[VMEM, VMEM],
        out_specs=VMEM,
        out_shape=blocks_of(32),
        compiler_params=pltpu.CompilerParams(vmem_limit_bytes=VMEM_LIMIT),
        name="interleave",
    )(mine, other)


def dot01(a, b):
    return jnp.dot(a.astype(F32).astype(BF16), b.astype(F32).astype(BF16), preferred_element_type=F32)


def dot01t(a, b):
    a, b = a.astype(F32).astype(BF16), b.astype(F32).astype(BF16)
    return lax.dot_general(a, b, (((1,), (1,)), ((), ())), preferred_element_type=F32)


def iota(shape, dim):
    return lax.broadcasted_iota(jnp.int32, shape, dim)


def along(value):
    return jnp.sum(value, axis=1, keepdims=True)


def zz(k):
    return (k & 31) >> 3


def yy(k):
    return (k & 7) >> 1


def tables(pattern, keep_square, keep_next):
    def kernel(pattern_ref, square_ref, next_ref, square_out, next_out, info_out):
        layer, row, col = lax.axis_index("layer"), lax.axis_index("row"), lax.axis_index("col")
        core, x = col & 1, row * 2 + layer
        z, y = zz(col), yy(col)
        pat = pattern_ref[...].astype(F32)
        keep = square_ref[...].astype(F32)
        keep2 = next_ref[...].astype(F32)
        i, k = iota((64, 64), 0), iota((64, 64), 1)
        parity = (i & 1) == (k & 1)
        even = (k & 1) == 0
        same_z, same_y = zz(i) == zz(k), yy(i) == yy(k)
        group = ((i & 31) == (k & 31)).astype(F32)

        g, g_k = iota((8, 64), 0), iota((8, 64), 1)
        owner = ((g_k >> 5) == (g >> 1)) & ((g_k & 1) == (g & 1))
        counts = dot01(owner, pat)
        ring = parity & ((even & same_z) | (~even & same_y))
        need = (
            jnp.max(dot01((g_k >> 5) == g, pat)),
            jnp.max(counts),
            jnp.max(dot01(counts, group)),
            jnp.max(dot01(counts, ring)),
            jnp.max(dot01(dot01(owner, keep), group)),
        )
        fits = need[0] <= TIERS[0][0]
        for a, b in zip(need[1:], TIERS[0][1:], strict=True):
            fits = fits & (a <= b)
        half, _, _, c2, c3 = [jnp.where(fits, a, b).astype(jnp.int32) for a, b in zip(*TIERS, strict=True)]

        o, kk = iota((32, 64), 0), iota((32, 64), 1)
        j = o >> 4
        p, q = iota((32, 32), 0), iota((32, 32), 1)
        same_j = (p >> 4) == (q >> 4)
        rowsel = (kk == row * 32 + 2 * (o & 15) + layer).astype(F32)
        colsel = (kk == j * 32 + col).astype(F32)
        rows = dot01(rowsel, pat)
        cols = dot01t(colsel, pat)
        kept = dot01t(colsel, keep)
        keep_mine = along(kept * rowsel)
        next_mine = along(dot01(rowsel, keep2) * colsel)

        column_count = dot01(same_j, rows)
        rank1 = dot01(same_j & (q < p), rows) + dot01(column_count, i == k - 32)
        before = parity & ((even & same_z & (yy(i) < yy(k))) | (~even & same_y & (zz(i) < zz(k))))
        offset = dot01(column_count, before)
        number = dot01(column_count, group)
        distance = jnp.where((kk & 1) == 0, zz(kk) - z, yy(kk) - y) & 3
        slot_left = distance * c2 + jnp.where((kk & 1) == core, 0, 4 * c2) + (offset + rank1).astype(jnp.int32)
        nothing_left = 8 * c2

        def place(x_other):
            e = (x_other - x) & 3
            return jnp.where(core == 0, (4 - e) & 3, e)

        rank0 = dot01(cols, ((i >> 5) == (k >> 5)) & (i < k))
        slot_right = place((kk >> 5) * 2 + j) * half + rank0.astype(jnp.int32)
        both = dot01((p & 15) == (q & 15), kept)
        first = dot01(q == (p & 15), kept)
        rank3 = dot01(both, parity & ((i >> 5) == (k >> 5)) & (i < k)) + jnp.where(j == 1, first, 0.0)
        slot_square = place((kk >> 5) * 2 + (kk & 1)) * c3 + rank3.astype(jnp.int32)

        lane = iota((32, 128), 1)

        def listed(hit, right, nothing_right):
            rank = dot01(hit, i < k)
            rank = jnp.where(hit > 0, rank, -1.0).astype(jnp.int32)
            code = ((slot_left << SHIFT) + right).astype(F32)
            number = along(hit)
            nothing = ((nothing_left << SHIFT) + nothing_right).astype(F32)

            def step(n, out):
                value = along(jnp.where(rank == n, code, 0.0))
                value = jnp.where(number > n.astype(F32), value, nothing)
                return jnp.where(lane == n, value, out)

            most = jnp.max(number).astype(jnp.int32)
            out = lax.fori_loop(0, most, step, jnp.full((32, 128), 1.0, F32) * nothing)
            return jnp.where(lane == 64, number, out)

        square = listed(rows * cols * keep_mine, slot_right, 4 * half)
        square = jnp.where(lane == 65, keep_mine, square)
        square = jnp.where(lane == 66, along(rank3 * rowsel), square)
        square_out[...] = square.astype(jnp.int32)

        following = listed(rows * kept * next_mine, slot_square, 4 * c3)
        following = jnp.where(lane == 65, next_mine, following)
        start = along(jnp.where(colsel * rows > 0, slot_left - nothing_left, 0).astype(F32))
        following = jnp.where(lane == 66, start + nothing_left.astype(F32), following)
        mine = (q == layer * 16).astype(F32)
        own_slot = dot01(mine, slot_square)
        own_kept = dot01(mine, kept)
        here = (kk == row * 32 + o).astype(F32)
        own = along(here * own_kept * (own_slot + 1.0)) - 1.0
        following = jnp.where(lane == 67, own, following)
        next_out[...] = following.astype(jnp.int32)

        target = jnp.where(core == 0, z * 8 + ((y + g) & 3) * 2, ((z + g) & 3) * 8 + y * 2 + 1)
        ring_sel = (g_k == target).astype(F32)
        ring_number = along(ring_sel * number[:8])
        ring_offset = along(ring_sel * offset[:8])
        lane8 = iota((8, 128), 1)
        info = jnp.where(lane8 == 1, ring_number, jnp.where(lane8 == 2, ring_offset, jnp.where(fits, 0.0, 1.0)))
        info_out[...] = info.astype(jnp.int32)

    return pl.pallas_call(
        kernel,
        in_specs=[VMEM] * 3,
        out_specs=[VMEM] * 3,
        out_shape=[jax.ShapeDtypeStruct((n, 128), jnp.int32) for n in (32, 32, 8)],
        name="tables",
    )(pattern, keep_square, keep_next)


def first_half(caps, values, pattern):
    own, sent = pack_column(pattern, values, caps[0], caps[1])
    return own, swap_layer(sent)


def packed(caps, values, pattern, own, received, square_list, next_list, info):
    half, part, c1, c2, c3 = caps
    if own.shape[0] != half * TILE or received.shape[0] != part * TILE:
        own, received = first_half(caps, values, pattern)

    with jax.named_scope("left_chunk"):
        chunk = pack_rows(pattern, values, received, c1)
        chunks = [chunk] + [shift_ring(chunk, -e, 0) for e in (1, 2, 3)]
    with jax.named_scope("right_columns"):
        carried = carry_x(after(own, chunk))
        *chunks, carried = lax.optimization_barrier((*chunks, carried))
        crossed, carried2 = carry_x(after(swap_core(own), chunks[1])), carry_x(carried)
    with jax.named_scope("left_rows"):
        ring = pack_ring(info, chunks, c2)
        ring3, ring1 = shift_ring(ring, 1, 1), shift_ring(ring, -1, 1)
        middle = c2 // 2 * TILE
        lo2, hi2 = shift_ring(ring3[:middle], 1, 1), shift_ring(ring1[middle:], -1, 1)
        rings = [ring, ring1, lo2, hi2, ring3]
        lefts = rings + [swap_core(v) for v in rings]
    with jax.named_scope("right_columns"):
        rights = [own, carried, carried2, swap_core(crossed)]
    with jax.named_scope("square"):
        squares = gather_x(square_blocks(square_list, lefts, rights, c3))
    with jax.named_scope("next"):
        (sent,) = next_blocks(next_list, lefts, squares, False)
        other = swap_layer(sent)
        mine, square = next_blocks(next_list, lefts, squares, True)
        next_sign = interleave(mine, other)
    return (square, next_sign)


def local(values, pattern, keep_square, keep_next):
    own, received = first_half(TIERS[0], values, pattern)
    square_list, next_list, info = tables(pattern, keep_square, keep_next)
    branches = [functools.partial(packed, caps) for caps in TIERS]
    return lax.switch(info[0, 0], branches, values, pattern, own, received, square_list, next_list, info)


def solution(mesh):
    return jax.shard_map(
        local,
        mesh=mesh,
        in_specs=(P("row", ("layer", "col")), P(), P(), P()),
        out_specs=(P("row", ("layer", "col")), P("row", ("layer", "col"))),
        check_vma=False,
    )
```

```python
import functools

import jax
import jax.numpy as jnp
from jax import lax
from jax.experimental import pallas as pl
from jax.experimental.pallas import tpu as pltpu
from jax.sharding import PartitionSpec as P

TILE = 128
SHIFT = 10
MASK = (1 << SHIFT) - 1
BF16 = jnp.bfloat16
F32 = jnp.float32
TIERS = ((18, 11, 12, 34, 16), (18, 11, 14, 38, 18), (32, 16, 32, 128, 32))
VMEM_LIMIT = 20 * 1024 * 1024


def shift_ring(value, by, stage):
    def target(c):
        z, y, core = c // 8, c // 2 % 4, c % 2
        if core == stage:
            y = (y + by) % 4
        else:
            z = (z + by) % 4
        return z * 8 + y * 2 + core

    return lax.ppermute(value, "col", [(c, target(c)) for c in range(32)])


def carry_x(value):
    def target(i):
        layer, row, col = i // 64, i // 32 % 2, i % 32
        x = (row * 2 + layer + (1 if col % 2 == 0 else -1)) % 4
        return x % 2 * 64 + x // 2 * 32 + col

    return lax.ppermute(value, ("layer", "row", "col"), [(i, target(i)) for i in range(128)])


def gather_x(value):
    carried = carry_x(value)
    crossed = carry_x(swap_core(value))
    return [value, carried, carry_x(carried), swap_core(crossed)]


def place_x(x, e, core):
    return jnp.where(core == 0, (4 - e) % 4, e)


def swap_core(value):
    return lax.ppermute(value, "col", [(c, c ^ 1) for c in range(32)])


def swap_layer(value):
    return lax.ppermute(value, "layer", [(0, 1), (1, 0)])


def after(value, *others):
    return lax.optimization_barrier((value, *others))[0]


def blocks_of(count):
    return jax.ShapeDtypeStruct((count * TILE, TILE), BF16)


def at_block(index):
    return pl.ds(pl.multiple_of(index * TILE, TILE), TILE)


ANY = pl.BlockSpec(memory_space=pl.ANY)
VMEM = pl.BlockSpec(memory_space=pltpu.VMEM)


def fetch(sources, offsets, scratch, sems):
    copies = [
        pltpu.make_async_copy(src, scratch.at[pl.ds(off * TILE, src.shape[0])], sems.at[n])
        for n, (src, off) in enumerate(zip(sources, offsets, strict=True))
    ]
    for copy in copies:
        copy.start()
    return copies


def offsets_of(arrays):
    offsets, total = [], 0
    for a in arrays:
        offsets.append(total)
        total += a.shape[0] // TILE
    return offsets, total


def pack_column(pattern, values, half, part):
    def kernel(pattern_ref, values_ref, own_ref, sent_ref):
        layer = lax.axis_index("layer")
        first = lax.axis_index("row") * 32
        column = layer * 32 + lax.axis_index("col")

        def step(a, counts):
            n, m = counts
            for s in range(2):
                t = 2 * a + s
                keep = pattern_ref[first + t, column]

                @pl.when((keep != 0) & (n < half))
                def _(n=n, t=t):
                    own_ref[at_block(n), :] = values_ref[at_block(t), :]

                @pl.when((keep != 0) & (m < part) & (layer != s))
                def _(m=m, t=t):
                    sent_ref[at_block(m), :] = values_ref[at_block(t), :]

                n = n + keep
                m = m + jnp.where(layer != s, keep, 0)
            return n, m

        lax.fori_loop(0, 16, step, (0, 0))

    return pl.pallas_call(
        kernel,
        grid_spec=pltpu.PrefetchScalarGridSpec(
            num_scalar_prefetch=1, grid=(), in_specs=[VMEM], out_specs=[VMEM, VMEM]),
        out_shape=[blocks_of(half), blocks_of(part)],
        compiler_params=pltpu.CompilerParams(vmem_limit_bytes=VMEM_LIMIT),
        name="pack_column",
    )(pattern, values)


def pack_rows(pattern, values, received, cap):
    def kernel(pattern_ref, values_ref, received_ref, out_ref):
        layer = lax.axis_index("layer")
        first = lax.axis_index("row") * 32 + layer
        col = lax.axis_index("col")
        count = lax.fori_loop(0, 16, lambda a, n: n + pattern_ref[first + 2 * a, (1 - layer) * 32 + col], 0, unroll=4)

        def step(a, n):
            keep = pattern_ref[first + 2 * a, layer * 32 + col]

            @pl.when((keep != 0) & (n < cap))
            def _():
                out_ref[at_block(n), :] = values_ref[at_block(2 * a + layer), :]

            return n + keep

        end = lax.fori_loop(0, 16, step, jnp.where(layer == 0, 0, count))
        base = jnp.where(layer == 0, end, 0)

        def copy(n, carry):
            out_ref[at_block(base + n), :] = received_ref[at_block(n), :]
            return carry

        lax.fori_loop(0, jnp.minimum(count, cap - base), copy, 0)

    return pl.pallas_call(
        kernel,
        grid_spec=pltpu.PrefetchScalarGridSpec(
            num_scalar_prefetch=1, grid=(), in_specs=[VMEM, VMEM], out_specs=VMEM),
        out_shape=blocks_of(cap),
        compiler_params=pltpu.CompilerParams(vmem_limit_bytes=VMEM_LIMIT),
        name="pack_rows",
    )(pattern, values, received)


def pack_ring(info, chunks, cap):
    cut = chunks[2].shape[0] // TILE
    parts = ((0, 0), (1, 0), (2, 0), (2, cut), (3, 0))

    def kernel(info_ref, *refs):
        out = refs[5]
        for (e, skip), ref in zip(parts, refs[:5], strict=True):
            first, number = info_ref[e, 2] + skip, info_ref[e, 1] - skip

            def copy(n, carry, ref=ref, first=first):
                out[at_block(jnp.minimum(first + n, cap - 1)), :] = ref[at_block(n), :]
                return carry

            lax.fori_loop(0, jnp.minimum(number, ref.shape[0] // TILE), copy, 0)

    return pl.pallas_call(
        kernel,
        grid_spec=pltpu.PrefetchScalarGridSpec(
            num_scalar_prefetch=1, grid=(), in_specs=[VMEM] * 5, out_specs=VMEM),
        out_shape=blocks_of(cap),
        compiler_params=pltpu.CompilerParams(vmem_limit_bytes=VMEM_LIMIT),
        name="pack_ring",
    )(info, *chunks)


def sum_of_products(row, list_ref, count, left, right):
    def step(i, total):
        codes = [list_ref[row, i * 4 + u] for u in range(4)]
        a = jnp.concatenate([left[at_block(c >> SHIFT), :] for c in codes], axis=1)
        b = jnp.concatenate([right[at_block(c & MASK), :] for c in codes], axis=0)
        return total + jnp.dot(a, b, preferred_element_type=F32)

    return lax.fori_loop(0, (count + 3) >> 2, step, jnp.zeros((TILE, TILE), F32))


def vmem_for(blocks):
    return blocks * TILE * TILE * 2 + 6 * 1024 * 1024


def load_operands(left_srcs, right_srcs, left_offs, right_offs, left, right, sems):
    n = len(left_srcs)
    copies = fetch(left_srcs, left_offs, left, sems)
    copies += fetch(right_srcs, right_offs, right, sems.at[pl.ds(n, len(right_srcs))])
    zero = jnp.zeros((TILE, TILE), BF16)
    if left is not None:
        left[pl.ds(left.shape[0] - TILE, TILE), :] = zero
    right[pl.ds(right.shape[0] - TILE, TILE), :] = zero
    for copy in copies:
        copy.wait()


def store_of(blocks):
    shape = (blocks * TILE, TILE)
    return pltpu.VMEM(shape, BF16) if blocks <= 400 else jax.ShapeDtypeStruct(shape, BF16)


def square_blocks(lists, lefts, rights, cap):
    left_offs, left_total = offsets_of(lefts)
    right_offs, right_total = offsets_of(rights)
    nl, nr = len(lefts), len(rights)

    def kernel(list_ref, *refs):
        out, left, right, sems = refs[nl + nr :]
        load_operands(refs[:nl], refs[nl : nl + nr], left_offs, right_offs, left, right, sems)

        def step(o, carry):
            @pl.when(list_ref[o, 65] != 0)
            def _():
                total = sum_of_products(o, list_ref, list_ref[o, 64], left, right)
                out[at_block(jnp.minimum(list_ref[o, 66], cap - 1)), :] = total.astype(BF16)

            return carry

        lax.fori_loop(0, 32, step, 0)

    return pl.pallas_call(
        kernel,
        grid_spec=pltpu.PrefetchScalarGridSpec(
            num_scalar_prefetch=1, grid=(), in_specs=[ANY] * (nl + nr), out_specs=[VMEM, VMEM],
            scratch_shapes=[
                pltpu.VMEM(((right_total + 1) * TILE, TILE), BF16),
                pltpu.SemaphoreType.DMA((nl + nr,)),
            ]),
        out_shape=[blocks_of(cap), store_of(left_total + 1)],
        compiler_params=pltpu.CompilerParams(vmem_limit_bytes=vmem_for(left_total + right_total)),
        name="square_blocks",
    )(lists, *lefts, *rights)


def next_blocks(lists, left, rights, own):
    right_offs, right_total = offsets_of(rights)
    nr = len(rights)
    n_out = 2 if own else 1

    def kernel(list_ref, *refs):
        left, outs = refs[0], refs[1 + nr : 1 + nr + n_out]
        right, sems = refs[1 + nr + n_out :]
        load_operands((), refs[1 : 1 + nr], (), right_offs, None, right, sems)
        layer = lax.axis_index("layer")
        column = layer if own else 1 - layer

        def step(a, carry):
            o = column * 16 + a
            outs[0][at_block(a), :] = jnp.zeros((TILE, TILE), BF16)

            @pl.when(list_ref[o, 65] != 0)
            def _():
                total = sum_of_products(o, list_ref, list_ref[o, 64], left, right)
                start = left[at_block(list_ref[o, 66]), :].astype(F32)
                outs[0][at_block(a), :] = (1.5 * start - 0.5 * total).astype(BF16)

            return carry

        lax.fori_loop(0, 16, step, 0)

        if own:
            def place(t, carry):
                slot = list_ref[t, 67]

                @pl.when(slot >= 0)
                def _():
                    outs[1][at_block(t), :] = right[at_block(slot), :]

                @pl.when(slot < 0)
                def _():
                    outs[1][at_block(t), :] = jnp.zeros((TILE, TILE), BF16)

                return carry

            lax.fori_loop(0, 32, place, 0)

    return pl.pallas_call(
        kernel,
        grid_spec=pltpu.PrefetchScalarGridSpec(
            num_scalar_prefetch=1, grid=(), in_specs=[VMEM] + [ANY] * nr, out_specs=[VMEM] * n_out,
            scratch_shapes=[
                pltpu.VMEM(((right_total + 1) * TILE, TILE), BF16),
                pltpu.SemaphoreType.DMA((nr,)),
            ]),
        out_shape=[blocks_of(16)] + ([blocks_of(32)] if own else []),
        compiler_params=pltpu.CompilerParams(vmem_limit_bytes=vmem_for(right_total + left.shape[0] // TILE)),
        name="next_own" if own else "next_sent",
    )(lists, left, *rights)


def interleave(mine, other):
    def kernel(mine_ref, other_ref, out_ref):
        layer = lax.axis_index("layer")
        for a in range(16):
            out_ref[at_block(2 * a + layer), :] = mine_ref[pl.ds(a * TILE, TILE), :]
            out_ref[at_block(2 * a + 1 - layer), :] = other_ref[pl.ds(a * TILE, TILE), :]

    return pl.pallas_call(
        kernel,
        in_specs=[VMEM, VMEM],
        out_specs=VMEM,
        out_shape=blocks_of(32),
        compiler_params=pltpu.CompilerParams(vmem_limit_bytes=VMEM_LIMIT),
        name="interleave",
    )(mine, other)


def dot01(a, b):
    return jnp.dot(a.astype(F32).astype(BF16), b.astype(F32).astype(BF16), preferred_element_type=F32)


def dot01t(a, b):
    a, b = a.astype(F32).astype(BF16), b.astype(F32).astype(BF16)
    return lax.dot_general(a, b, (((1,), (1,)), ((), ())), preferred_element_type=F32)


def iota(shape, dim):
    return lax.broadcasted_iota(jnp.int32, shape, dim)


def along(value):
    return jnp.sum(value, axis=1, keepdims=True)


def zz(k):
    return (k & 31) >> 3


def yy(k):
    return (k & 7) >> 1


def tables(pattern, keep_square, keep_next):
    def kernel(pattern_ref, square_ref, next_ref, square_out, next_out, info_out):
        layer, row, col = lax.axis_index("layer"), lax.axis_index("row"), lax.axis_index("col")
        core, x = col & 1, row * 2 + layer
        z, y = zz(col), yy(col)
        pat = pattern_ref[...].astype(F32)
        keep = square_ref[...].astype(F32)
        keep2 = next_ref[...].astype(F32)
        i, k = iota((64, 64), 0), iota((64, 64), 1)
        parity = (i & 1) == (k & 1)
        even = (k & 1) == 0
        same_z, same_y = zz(i) == zz(k), yy(i) == yy(k)
        group = ((i & 31) == (k & 31)).astype(F32)

        g, g_k = iota((8, 64), 0), iota((8, 64), 1)
        owner = ((g_k >> 5) == (g >> 1)) & ((g_k & 1) == (g & 1))
        counts = dot01(owner, pat)
        ring = parity & ((even & same_z) | (~even & same_y))
        need = (
            jnp.max(dot01((g_k >> 5) == g, pat)),
            jnp.max(counts),
            jnp.max(dot01(counts, group)),
            jnp.max(dot01(counts, ring)),
            jnp.max(dot01(dot01(owner, keep), group)),
        )
        fits = [functools.reduce(jnp.logical_and, [a <= b for a, b in zip(need, t, strict=True)]) for t in TIERS[:2]]

        def by_tier(a, b, c):
            return jnp.where(fits[0], a, jnp.where(fits[1], b, c)).astype(jnp.int32)

        half, _, _, c2, c3 = [by_tier(*caps) for caps in zip(*TIERS, strict=True)]
        tier = by_tier(0, 1, 2)

        o, kk = iota((32, 64), 0), iota((32, 64), 1)
        j = o >> 4
        p, q = iota((32, 32), 0), iota((32, 32), 1)
        same_j = (p >> 4) == (q >> 4)
        rowsel = (kk == row * 32 + 2 * (o & 15) + layer).astype(F32)
        colsel = (kk == j * 32 + col).astype(F32)
        rows = dot01(rowsel, pat)
        cols = dot01t(colsel, pat)
        kept = dot01t(colsel, keep)
        keep_mine = along(kept * rowsel)
        next_mine = along(dot01(rowsel, keep2) * colsel)

        column_count = dot01(same_j, rows)
        rank1 = dot01(same_j & (q < p), rows) + dot01(column_count, i == k - 32)
        before = parity & ((even & same_z & (yy(i) < yy(k))) | (~even & same_y & (zz(i) < zz(k))))
        offset = dot01(column_count, before)
        number = dot01(column_count, group)
        distance = jnp.where((kk & 1) == 0, zz(kk) - z, yy(kk) - y) & 3
        slot_left = distance * c2 + jnp.where((kk & 1) == core, 0, 4 * c2) + (offset + rank1).astype(jnp.int32)
        nothing_left = 8 * c2

        def place(x_other):
            e = (x_other - x) & 3
            return jnp.where(core == 0, (4 - e) & 3, e)

        rank0 = dot01(cols, ((i >> 5) == (k >> 5)) & (i < k))
        slot_right = place((kk >> 5) * 2 + j) * half + rank0.astype(jnp.int32)
        both = dot01((p & 15) == (q & 15), kept)
        first = dot01(q == (p & 15), kept)
        rank3 = dot01(both, parity & ((i >> 5) == (k >> 5)) & (i < k)) + jnp.where(j == 1, first, 0.0)
        slot_square = place((kk >> 5) * 2 + (kk & 1)) * c3 + rank3.astype(jnp.int32)

        lane = iota((32, 128), 1)

        def listed(hit, right, nothing_right):
            rank = dot01(hit, i < k)
            rank = jnp.where(hit > 0, rank, -1.0).astype(jnp.int32)
            code = ((slot_left << SHIFT) + right).astype(F32)
            number = along(hit)
            nothing = ((nothing_left << SHIFT) + nothing_right).astype(F32)

            def step(n, out):
                value = along(jnp.where(rank == n, code, 0.0))
                value = jnp.where(number > n.astype(F32), value, nothing)
                return jnp.where(lane == n, value, out)

            most = jnp.max(number).astype(jnp.int32)
            out = lax.fori_loop(0, most, step, jnp.full((32, 128), 1.0, F32) * nothing)
            return jnp.where(lane == 64, number, out)

        square = listed(rows * cols * keep_mine, slot_right, 4 * half)
        square = jnp.where(lane == 65, keep_mine, square)
        square = jnp.where(lane == 66, along(rank3 * rowsel), square)
        square_out[...] = square.astype(jnp.int32)

        following = listed(rows * kept * next_mine, slot_square, 4 * c3)
        following = jnp.where(lane == 65, next_mine, following)
        start = along(jnp.where(colsel * rows > 0, slot_left - nothing_left, 0).astype(F32))
        following = jnp.where(lane == 66, start + nothing_left.astype(F32), following)
        mine = (q == layer * 16).astype(F32)
        own_slot = dot01(mine, slot_square)
        own_kept = dot01(mine, kept)
        here = (kk == row * 32 + o).astype(F32)
        own = along(here * own_kept * (own_slot + 1.0)) - 1.0
        following = jnp.where(lane == 67, own, following)
        next_out[...] = following.astype(jnp.int32)

        target = jnp.where(core == 0, z * 8 + ((y + g) & 3) * 2, ((z + g) & 3) * 8 + y * 2 + 1)
        ring_sel = (g_k == target).astype(F32)
        ring_number = along(ring_sel * number[:8])
        ring_offset = along(ring_sel * offset[:8])
        lane8 = iota((8, 128), 1)
        info = jnp.where(lane8 == 1, ring_number, jnp.where(lane8 == 2, ring_offset, tier.astype(F32)))
        info_out[...] = info.astype(jnp.int32)

    return pl.pallas_call(
        kernel,
        in_specs=[VMEM] * 3,
        out_specs=[VMEM] * 3,
        out_shape=[jax.ShapeDtypeStruct((n, 128), jnp.int32) for n in (32, 32, 8)],
        name="tables",
    )(pattern, keep_square, keep_next)


def first_half(caps, values, pattern):
    own, sent = pack_column(pattern, values, caps[0], caps[1])
    return own, swap_layer(sent)


def packed(caps, values, pattern, own, received, square_list, next_list, info):
    half, part, c1, c2, c3 = caps
    if own.shape[0] != half * TILE or received.shape[0] != part * TILE:
        own, received = first_half(caps, values, pattern)

    with jax.named_scope("left_chunk"):
        chunk = pack_rows(pattern, values, received, c1)
        far, near = shift_ring(chunk, 1, 0), shift_ring(chunk, -1, 0)
        cut = c1 // 2 * TILE
        chunks = [chunk, near, shift_ring(far[:cut], 1, 0), shift_ring(near[cut:], -1, 0), far]
    with jax.named_scope("right_columns"):
        carried = carry_x(after(own, chunk))
        *chunks, carried = lax.optimization_barrier((*chunks, carried))
        crossed, carried2 = carry_x(after(swap_core(own), near)), carry_x(carried)
    with jax.named_scope("left_rows"):
        ring = pack_ring(info, chunks, c2)
        ring3, ring1 = shift_ring(ring, 1, 1), shift_ring(ring, -1, 1)
        middle = c2 // 2 * TILE
        lo2, hi2 = shift_ring(ring3[:middle], 1, 1), shift_ring(ring1[middle:], -1, 1)
        rings = [ring, ring1, lo2, hi2, ring3]
        lefts = rings + [swap_core(v) for v in rings]
    with jax.named_scope("right_columns"):
        rights = [own, carried, carried2, swap_core(crossed)]
    with jax.named_scope("square"):
        kept, left = square_blocks(square_list, lefts, rights, c3)
        squares = gather_x(kept)
    with jax.named_scope("next"):
        (sent,) = next_blocks(next_list, left, squares, False)
        other = swap_layer(sent)
        mine, square = next_blocks(next_list, left, squares, True)
        next_sign = interleave(mine, other)
    return (square, next_sign)


def local(values, pattern, keep_square, keep_next):
    own, received = first_half(TIERS[0], values, pattern)
    square_list, next_list, info = tables(pattern, keep_square, keep_next)
    tier = info[0, 0]
    first, second, last = [functools.partial(packed, caps) for caps in TIERS]

    def others(*args):
        return lax.cond(tier == 1, second, last, *args)

    return lax.cond(tier == 0, first, others, values, pattern, own, received, square_list, next_list, info)


def solution(mesh):
    return jax.shard_map(
        local,
        mesh=mesh,
        in_specs=(P("row", ("layer", "col")), P(), P(), P()),
        out_specs=(P("row", ("layer", "col")), P("row", ("layer", "col"))),
        check_vma=False,
    )
```

```python
import functools

import jax
import jax.numpy as jnp
from jax import lax
from jax.experimental import pallas as pl
from jax.experimental.pallas import tpu as pltpu
from jax.sharding import PartitionSpec as P

TILE = 128
SHIFT = 10
MASK = (1 << SHIFT) - 1
BF16 = jnp.bfloat16
F32 = jnp.float32
TIERS = ((18, 11, 12, 34, 16), (18, 11, 14, 38, 18), (32, 16, 32, 128, 32))
VMEM_LIMIT = 20 * 1024 * 1024


def shift_ring(value, by, stage):
    def target(c):
        z, y, core = c // 8, c // 2 % 4, c % 2
        if core == stage:
            y = (y + by) % 4
        else:
            z = (z + by) % 4
        return z * 8 + y * 2 + core

    return lax.ppermute(value, "col", [(c, target(c)) for c in range(32)])


def carry_x(value):
    def target(i):
        layer, row, col = i // 64, i // 32 % 2, i % 32
        x = (row * 2 + layer + (1 if col % 2 == 0 else -1)) % 4
        return x % 2 * 64 + x // 2 * 32 + col

    return lax.ppermute(value, ("layer", "row", "col"), [(i, target(i)) for i in range(128)])


def gather_x(value):
    carried = carry_x(value)
    crossed = carry_x(swap_core(value))
    return [value, carried, carry_x(carried), swap_core(crossed)]


def place_x(x, e, core):
    return jnp.where(core == 0, (4 - e) % 4, e)


def swap_core(value):
    return lax.ppermute(value, "col", [(c, c ^ 1) for c in range(32)])


def swap_layer(value):
    return lax.ppermute(value, "layer", [(0, 1), (1, 0)])


def after(value, *others):
    return lax.optimization_barrier((value, *others))[0]


def blocks_of(count):
    return jax.ShapeDtypeStruct((count * TILE, TILE), BF16)


def at_block(index):
    return pl.ds(pl.multiple_of(index * TILE, TILE), TILE)


ANY = pl.BlockSpec(memory_space=pl.ANY)
VMEM = pl.BlockSpec(memory_space=pltpu.VMEM)


def fetch(sources, offsets, scratch, sems):
    copies = [
        pltpu.make_async_copy(src, scratch.at[pl.ds(off * TILE, src.shape[0])], sems.at[n])
        for n, (src, off) in enumerate(zip(sources, offsets, strict=True))
    ]
    for copy in copies:
        copy.start()
    return copies


def offsets_of(arrays):
    offsets, total = [], 0
    for a in arrays:
        offsets.append(total)
        total += a.shape[0] // TILE
    return offsets, total


def pack_column(pattern, values, cap, sent):
    def kernel(pattern_ref, values_ref, out_ref):
        layer = lax.axis_index("layer")
        first = lax.axis_index("row") * 32
        column = layer * 32 + lax.axis_index("col")

        def step(a, n):
            t = 2 * a + 1 - layer if sent else a
            keep = pattern_ref[first + t, column]

            @pl.when((keep != 0) & (n < cap))
            def _():
                out_ref[at_block(n), :] = values_ref[at_block(t), :]

            return n + keep

        lax.fori_loop(0, 16 if sent else 32, step, 0, unroll=4)

    return pl.pallas_call(
        kernel,
        grid_spec=pltpu.PrefetchScalarGridSpec(
            num_scalar_prefetch=1, grid=(), in_specs=[VMEM], out_specs=VMEM),
        out_shape=blocks_of(cap),
        compiler_params=pltpu.CompilerParams(vmem_limit_bytes=VMEM_LIMIT),
        name="pack_sent" if sent else "pack_own",
    )(pattern, values)


def pack_rows(pattern, values, received, cap):
    def kernel(pattern_ref, values_ref, received_ref, out_ref):
        layer = lax.axis_index("layer")
        first = lax.axis_index("row") * 32 + layer
        col = lax.axis_index("col")
        count = lax.fori_loop(0, 16, lambda a, n: n + pattern_ref[first + 2 * a, (1 - layer) * 32 + col], 0, unroll=4)

        def step(a, n):
            keep = pattern_ref[first + 2 * a, layer * 32 + col]

            @pl.when((keep != 0) & (n < cap))
            def _():
                out_ref[at_block(n), :] = values_ref[at_block(2 * a + layer), :]

            return n + keep

        end = lax.fori_loop(0, 16, step, jnp.where(layer == 0, 0, count))
        base = jnp.where(layer == 0, end, 0)

        def copy(n, carry):
            out_ref[at_block(base + n), :] = received_ref[at_block(n), :]
            return carry

        lax.fori_loop(0, jnp.minimum(count, cap - base), copy, 0)

    return pl.pallas_call(
        kernel,
        grid_spec=pltpu.PrefetchScalarGridSpec(
            num_scalar_prefetch=1, grid=(), in_specs=[VMEM, VMEM], out_specs=VMEM),
        out_shape=blocks_of(cap),
        compiler_params=pltpu.CompilerParams(vmem_limit_bytes=VMEM_LIMIT),
        name="pack_rows",
    )(pattern, values, received)


def pack_ring(info, chunks, cap):
    cut = chunks[2].shape[0] // TILE
    parts = ((0, 0), (1, 0), (2, 0), (2, cut), (3, 0))

    def kernel(info_ref, *refs):
        out = refs[5]
        for (e, skip), ref in zip(parts, refs[:5], strict=True):
            first, number = info_ref[e, 2] + skip, info_ref[e, 1] - skip

            def copy(n, carry, ref=ref, first=first):
                out[at_block(jnp.minimum(first + n, cap - 1)), :] = ref[at_block(n), :]
                return carry

            lax.fori_loop(0, jnp.minimum(number, ref.shape[0] // TILE), copy, 0)

    return pl.pallas_call(
        kernel,
        grid_spec=pltpu.PrefetchScalarGridSpec(
            num_scalar_prefetch=1, grid=(), in_specs=[VMEM] * 5, out_specs=VMEM),
        out_shape=blocks_of(cap),
        compiler_params=pltpu.CompilerParams(vmem_limit_bytes=VMEM_LIMIT),
        name="pack_ring",
    )(info, *chunks)


def sum_of_products(row, list_ref, count, left, right):
    def step(i, total):
        codes = [list_ref[row, i * 4 + u] for u in range(4)]
        a = jnp.concatenate([left[at_block(c >> SHIFT), :] for c in codes], axis=1)
        b = jnp.concatenate([right[at_block(c & MASK), :] for c in codes], axis=0)
        return total + jnp.dot(a, b, preferred_element_type=F32)

    return lax.fori_loop(0, (count + 3) >> 2, step, jnp.zeros((TILE, TILE), F32))


def vmem_for(blocks):
    return blocks * TILE * TILE * 2 + 6 * 1024 * 1024


def load_operands(left_srcs, right_srcs, left_offs, right_offs, left, right, sems):
    n = len(left_srcs)
    copies = fetch(left_srcs, left_offs, left, sems)
    copies += fetch(right_srcs, right_offs, right, sems.at[pl.ds(n, len(right_srcs))])
    zero = jnp.zeros((TILE, TILE), BF16)
    if left is not None:
        left[pl.ds(left.shape[0] - TILE, TILE), :] = zero
    right[pl.ds(right.shape[0] - TILE, TILE), :] = zero
    for copy in copies:
        copy.wait()


def store_of(blocks):
    shape = (blocks * TILE, TILE)
    return pltpu.VMEM(shape, BF16) if blocks <= 400 else jax.ShapeDtypeStruct(shape, BF16)


def square_blocks(lists, lefts, rights, cap):
    left_offs, left_total = offsets_of(lefts)
    right_offs, right_total = offsets_of(rights)
    nl, nr = len(lefts), len(rights)

    def kernel(list_ref, *refs):
        out, left, right, sems = refs[nl + nr :]
        load_operands(refs[:nl], refs[nl : nl + nr], left_offs, right_offs, left, right, sems)

        def step(o, carry):
            @pl.when(list_ref[o, 65] != 0)
            def _():
                total = sum_of_products(o, list_ref, list_ref[o, 64], left, right)
                out[at_block(jnp.minimum(list_ref[o, 66], cap - 1)), :] = total.astype(BF16)

            return carry

        lax.fori_loop(0, 32, step, 0)

    return pl.pallas_call(
        kernel,
        grid_spec=pltpu.PrefetchScalarGridSpec(
            num_scalar_prefetch=1, grid=(), in_specs=[ANY] * (nl + nr), out_specs=[VMEM, VMEM],
            scratch_shapes=[
                pltpu.VMEM(((right_total + 1) * TILE, TILE), BF16),
                pltpu.SemaphoreType.DMA((nl + nr,)),
            ]),
        out_shape=[blocks_of(cap), store_of(left_total + 1)],
        compiler_params=pltpu.CompilerParams(vmem_limit_bytes=vmem_for(left_total + right_total)),
        name="square_blocks",
    )(lists, *lefts, *rights)


def next_blocks(lists, left, rights, own):
    right_offs, right_total = offsets_of(rights)
    nr = len(rights)
    n_out = 2 if own else 1

    def kernel(list_ref, *refs):
        left, outs = refs[0], refs[1 + nr : 1 + nr + n_out]
        right, sems = refs[1 + nr + n_out :]
        load_operands((), refs[1 : 1 + nr], (), right_offs, None, right, sems)
        layer = lax.axis_index("layer")
        column = layer if own else 1 - layer

        def step(a, carry):
            o = column * 16 + a
            outs[0][at_block(a), :] = jnp.zeros((TILE, TILE), BF16)

            @pl.when(list_ref[o, 65] != 0)
            def _():
                total = sum_of_products(o, list_ref, list_ref[o, 64], left, right)
                start = left[at_block(list_ref[o, 66]), :].astype(F32)
                outs[0][at_block(a), :] = (1.5 * start - 0.5 * total).astype(BF16)

            return carry

        lax.fori_loop(0, 16, step, 0)

        if own:
            def place(t, carry):
                slot = list_ref[t, 67]

                @pl.when(slot >= 0)
                def _():
                    outs[1][at_block(t), :] = right[at_block(slot), :]

                @pl.when(slot < 0)
                def _():
                    outs[1][at_block(t), :] = jnp.zeros((TILE, TILE), BF16)

                return carry

            lax.fori_loop(0, 32, place, 0)

    return pl.pallas_call(
        kernel,
        grid_spec=pltpu.PrefetchScalarGridSpec(
            num_scalar_prefetch=1, grid=(), in_specs=[VMEM] + [ANY] * nr, out_specs=[VMEM] * n_out,
            scratch_shapes=[
                pltpu.VMEM(((right_total + 1) * TILE, TILE), BF16),
                pltpu.SemaphoreType.DMA((nr,)),
            ]),
        out_shape=[blocks_of(16)] + ([blocks_of(32)] if own else []),
        compiler_params=pltpu.CompilerParams(vmem_limit_bytes=vmem_for(right_total + left.shape[0] // TILE)),
        name="next_own" if own else "next_sent",
    )(lists, left, *rights)


def interleave(mine, other):
    def kernel(mine_ref, other_ref, out_ref):
        layer = lax.axis_index("layer")
        for a in range(16):
            out_ref[at_block(2 * a + layer), :] = mine_ref[pl.ds(a * TILE, TILE), :]
            out_ref[at_block(2 * a + 1 - layer), :] = other_ref[pl.ds(a * TILE, TILE), :]

    return pl.pallas_call(
        kernel,
        in_specs=[VMEM, VMEM],
        out_specs=VMEM,
        out_shape=blocks_of(32),
        compiler_params=pltpu.CompilerParams(vmem_limit_bytes=VMEM_LIMIT),
        name="interleave",
    )(mine, other)


def dot01(a, b):
    return jnp.dot(a.astype(F32).astype(BF16), b.astype(F32).astype(BF16), preferred_element_type=F32)


def dot01t(a, b):
    a, b = a.astype(F32).astype(BF16), b.astype(F32).astype(BF16)
    return lax.dot_general(a, b, (((1,), (1,)), ((), ())), preferred_element_type=F32)


def iota(shape, dim):
    return lax.broadcasted_iota(jnp.int32, shape, dim)


def along(value):
    return jnp.sum(value, axis=1, keepdims=True)


def zz(k):
    return (k & 31) >> 3


def yy(k):
    return (k & 7) >> 1


def tables(pattern, keep_square, keep_next):
    def kernel(pattern_ref, square_ref, next_ref, square_out, next_out, info_out):
        layer, row, col = lax.axis_index("layer"), lax.axis_index("row"), lax.axis_index("col")
        core, x = col & 1, row * 2 + layer
        z, y = zz(col), yy(col)
        pat = pattern_ref[...].astype(F32)
        keep = square_ref[...].astype(F32)
        keep2 = next_ref[...].astype(F32)
        i, k = iota((64, 64), 0), iota((64, 64), 1)
        parity = (i & 1) == (k & 1)
        even = (k & 1) == 0
        same_z, same_y = zz(i) == zz(k), yy(i) == yy(k)
        group = ((i & 31) == (k & 31)).astype(F32)

        g, g_k = iota((8, 64), 0), iota((8, 64), 1)
        owner = ((g_k >> 5) == (g >> 1)) & ((g_k & 1) == (g & 1))
        counts = dot01(owner, pat)
        ring = parity & ((even & same_z) | (~even & same_y))
        need = (
            jnp.max(dot01((g_k >> 5) == g, pat)),
            jnp.max(counts),
            jnp.max(dot01(counts, group)),
            jnp.max(dot01(counts, ring)),
            jnp.max(dot01(dot01(owner, keep), group)),
        )
        fits = [functools.reduce(jnp.logical_and, [a <= b for a, b in zip(need, t, strict=True)]) for t in TIERS[:2]]

        def by_tier(a, b, c):
            return jnp.where(fits[0], a, jnp.where(fits[1], b, c)).astype(jnp.int32)

        half, _, _, c2, c3 = [by_tier(*caps) for caps in zip(*TIERS, strict=True)]
        tier = by_tier(0, 1, 2)

        o, kk = iota((32, 64), 0), iota((32, 64), 1)
        j = o >> 4
        p, q = iota((32, 32), 0), iota((32, 32), 1)
        same_j = (p >> 4) == (q >> 4)
        rowsel = (kk == row * 32 + 2 * (o & 15) + layer).astype(F32)
        colsel = (kk == j * 32 + col).astype(F32)
        rows = dot01(rowsel, pat)
        cols = dot01t(colsel, pat)
        kept = dot01t(colsel, keep)
        keep_mine = along(kept * rowsel)
        next_mine = along(dot01(rowsel, keep2) * colsel)

        column_count = dot01(same_j, rows)
        rank1 = dot01(same_j & (q < p), rows) + dot01(column_count, i == k - 32)
        before = parity & ((even & same_z & (yy(i) < yy(k))) | (~even & same_y & (zz(i) < zz(k))))
        offset = dot01(column_count, before)
        number = dot01(column_count, group)
        distance = jnp.where((kk & 1) == 0, zz(kk) - z, yy(kk) - y) & 3
        slot_left = distance * c2 + jnp.where((kk & 1) == core, 0, 4 * c2) + (offset + rank1).astype(jnp.int32)
        nothing_left = 8 * c2

        def place(x_other):
            e = (x_other - x) & 3
            return jnp.where(core == 0, (4 - e) & 3, e)

        rank0 = dot01(cols, ((i >> 5) == (k >> 5)) & (i < k))
        slot_right = place((kk >> 5) * 2 + j) * half + rank0.astype(jnp.int32)
        both = dot01((p & 15) == (q & 15), kept)
        first = dot01(q == (p & 15), kept)
        rank3 = dot01(both, parity & ((i >> 5) == (k >> 5)) & (i < k)) + jnp.where(j == 1, first, 0.0)
        slot_square = place((kk >> 5) * 2 + (kk & 1)) * c3 + rank3.astype(jnp.int32)

        lane = iota((32, 128), 1)

        def listed(hit, right, nothing_right):
            rank = dot01(hit, i < k)
            rank = jnp.where(hit > 0, rank, -1.0).astype(jnp.int32)
            code = ((slot_left << SHIFT) + right).astype(F32)
            number = along(hit)
            nothing = ((nothing_left << SHIFT) + nothing_right).astype(F32)

            def step(n, out):
                value = along(jnp.where(rank == n, code, 0.0))
                value = jnp.where(number > n.astype(F32), value, nothing)
                return jnp.where(lane == n, value, out)

            most = jnp.max(number).astype(jnp.int32)
            out = lax.fori_loop(0, most, step, jnp.full((32, 128), 1.0, F32) * nothing)
            return jnp.where(lane == 64, number, out)

        square = listed(rows * cols * keep_mine, slot_right, 4 * half)
        square = jnp.where(lane == 65, keep_mine, square)
        square = jnp.where(lane == 66, along(rank3 * rowsel), square)
        square_out[...] = square.astype(jnp.int32)

        following = listed(rows * kept * next_mine, slot_square, 4 * c3)
        following = jnp.where(lane == 65, next_mine, following)
        start = along(jnp.where(colsel * rows > 0, slot_left - nothing_left, 0).astype(F32))
        following = jnp.where(lane == 66, start + nothing_left.astype(F32), following)
        mine = (q == layer * 16).astype(F32)
        own_slot = dot01(mine, slot_square)
        own_kept = dot01(mine, kept)
        here = (kk == row * 32 + o).astype(F32)
        own = along(here * own_kept * (own_slot + 1.0)) - 1.0
        following = jnp.where(lane == 67, own, following)
        next_out[...] = following.astype(jnp.int32)

        target = jnp.where(core == 0, z * 8 + ((y + g) & 3) * 2, ((z + g) & 3) * 8 + y * 2 + 1)
        ring_sel = (g_k == target).astype(F32)
        ring_number = along(ring_sel * number[:8])
        ring_offset = along(ring_sel * offset[:8])
        lane8 = iota((8, 128), 1)
        info = jnp.where(lane8 == 1, ring_number, jnp.where(lane8 == 2, ring_offset, tier.astype(F32)))
        info_out[...] = info.astype(jnp.int32)

    return pl.pallas_call(
        kernel,
        in_specs=[VMEM] * 3,
        out_specs=[VMEM] * 3,
        out_shape=[jax.ShapeDtypeStruct((n, 128), jnp.int32) for n in (32, 32, 8)],
        name="tables",
    )(pattern, keep_square, keep_next)


def first_half(caps, values, pattern):
    sent = pack_column(pattern, values, caps[1], True)
    return pack_column(after(pattern, sent), values, caps[0], False), swap_layer(sent)


def packed(caps, values, pattern, own, received, square_list, next_list, info):
    half, part, c1, c2, c3 = caps
    if own.shape[0] != half * TILE or received.shape[0] != part * TILE:
        own, received = first_half(caps, values, pattern)

    with jax.named_scope("left_chunk"):
        chunk = pack_rows(pattern, values, received, c1)
        far, near = shift_ring(chunk, 1, 0), shift_ring(chunk, -1, 0)
        cut = c1 // 2 * TILE
        chunks = [chunk, near, shift_ring(far[:cut], 1, 0), shift_ring(near[cut:], -1, 0), far]
    with jax.named_scope("right_columns"):
        carried = carry_x(after(own, chunk))
        *chunks, carried = lax.optimization_barrier((*chunks, carried))
        crossed, carried2 = carry_x(after(swap_core(own), near)), carry_x(carried)
    with jax.named_scope("left_rows"):
        ring = pack_ring(info, chunks, c2)
        ring3, ring1 = shift_ring(ring, 1, 1), shift_ring(ring, -1, 1)
        middle = c2 // 2 * TILE
        lo2, hi2 = shift_ring(ring3[:middle], 1, 1), shift_ring(ring1[middle:], -1, 1)
        rings = [ring, ring1, lo2, hi2, ring3]
        lefts = rings + [swap_core(v) for v in rings]
    with jax.named_scope("right_columns"):
        rights = [own, carried, carried2, swap_core(crossed)]
    with jax.named_scope("square"):
        kept, left = square_blocks(square_list, lefts, rights, c3)
        squares = gather_x(kept)
    with jax.named_scope("next"):
        (sent,) = next_blocks(next_list, left, squares, False)
        other = swap_layer(sent)
        mine, square = next_blocks(next_list, left, squares, True)
        next_sign = interleave(mine, other)
    return (square, next_sign)


def local(values, pattern, keep_square, keep_next):
    own, received = first_half(TIERS[0], values, pattern)
    square_list, next_list, info = tables(pattern, keep_square, keep_next)
    tier = info[0, 0]
    first, second, last = [functools.partial(packed, caps) for caps in TIERS]

    def others(*args):
        return lax.cond(tier == 1, second, last, *args)

    return lax.cond(tier == 0, first, others, values, pattern, own, received, square_list, next_list, info)


def solution(mesh):
    return jax.shard_map(
        local,
        mesh=mesh,
        in_specs=(P("row", ("layer", "col")), P(), P(), P()),
        out_specs=(P("row", ("layer", "col")), P("row", ("layer", "col"))),
        check_vma=False,
    )
```
